256 devices in a mesh: depth: 32 (over y, z), col: 8 (over x, core).
Axes of the slice: x: 4, y: 4, z: 8, core: 2. Of those that a mesh axis runs over, the one named last changes fastest.
Arguments:
- volume: float32 [512, 256, 2048], P('depth', None, 'col'), may hold values from -6 to 6
- tf_center: float32 [8], replicated, may hold values from -2.5 to 2.5
- tf_width: float32 [8], replicated, may hold values from 0.3 to 1.5
- tf_density: float32 [8], replicated, may hold values from 0.1 to 2
- tf_color: float32 [3, 8], replicated, may hold values from 0.05 to 1
- light: float32 [3], replicated, may hold values from 0.3 to 1
Outputs:
- image: float32 [4, 256, 2048], P(None, 'depth', 'col')
The draws below stay inside these ranges and needn't reach their ends.
All inputs are finite; a program needn't handle non-finite values.
Results may differ from the reference program's by a relative error of at most 0.00028.
Values sent between devices are 32-bit elements; how exact they have to be, the bound alone decides.
No kernel may reach another device: no remote copies, remote signals or barrier semaphores. Data moves between devices by JAX's collectives and lax.ppermute only.
A program may use at most 64 MiB of HBM per device.

```python
import math
import jax
import jax.numpy as jnp
from jax import lax

BUMPS = 8
NZ = 512
NY = 256
NX = 2048


def level_of(stream_key, extent, pieces, smallest, top_value):
    gain, own = 1.0, jax.random.fold_in(stream_key, 6)
    for dim, shards_of in pieces:
        heights = jnp.exp(jax.random.uniform(jax.random.fold_in(own, dim), (shards_of,), jnp.float32, smallest / len(pieces), top_value / len(pieces)))
        gain = gain * jnp.repeat(heights, extent[dim] // shards_of).reshape([-1 if axis == dim else 1 for axis in range(len(extent))])
    return gain


def centred(key, shape, spread, reach, cuts=(), held_as=jnp.bfloat16):
    array = jax.random.normal(key, shape, jnp.float32) * spread
    if len(cuts) > 0:
        array = level_of(key, shape, cuts, -0.22, 0.18) * array
    return jnp.clip(array, min=-reach, max=reach).astype(held_as)


def setup_inputs(seed: int = 0) -> dict:
    streams_of = jax.random.split(jax.random.key(seed), 7)
    return {
        "volume": centred(streams_of[0], (NZ, NY, NX), 1.0, 6.0, ((0, 32), (2, 8)), jnp.float32),
        "tf_center": jnp.clip(jax.random.uniform(streams_of[1], (BUMPS,), jnp.float32, -2.5, 2.5), -2.5, 2.5),
        "tf_width": jnp.clip(jnp.exp(jax.random.uniform(streams_of[2], (BUMPS,), jnp.float32, math.log(0.3), math.log(1.5))), 0.3, 1.5),
        "tf_density": jnp.clip(jnp.exp(jax.random.uniform(streams_of[3], (BUMPS,), jnp.float32, math.log(0.1), math.log(2.0))), 0.1, 2.0),
        "tf_color": jnp.clip(jax.random.uniform(streams_of[4], (3, BUMPS), jnp.float32, 0.05, 1.0), 0.05, 1.0),
        "light": jnp.clip(jax.random.uniform(streams_of[5], (3,), jnp.float32, 0.3, 1.0), 0.3, 1.0),
    }


def classify(cell, tf_center, tf_width, tf_density, tf_color):
    bumps = jnp.exp(-jnp.square((cell[None] - tf_center[:, None, None]) / tf_width[:, None, None]))
    ext = lax.optimization_barrier(jnp.sum(tf_density[:, None, None] * bumps, axis=0)) / NZ
    emit = jnp.einsum('ck,kyx->cyx', tf_color, bumps, precision=lax.Precision.HIGHEST)
    return (ext, emit)

def shading(below, cell, above, light):
    padded = jnp.pad(cell, 1)
    grad_x = (padded[1:-1, 2:] - padded[1:-1, :-2]) * 0.5
    grad_y = (padded[2:, 1:-1] - padded[:-2, 1:-1]) * 0.5
    grad_z = (above - below) * 0.5
    lit = jnp.abs(light[0] * grad_x + light[1] * grad_y + light[2] * grad_z)
    return 0.3 + 0.7 * lit / jnp.sqrt(grad_x * grad_x + grad_y * grad_y + grad_z * grad_z + 1.0)

def reference(volume, tf_center, tf_width, tf_density, tf_color, light):
    padded = jnp.pad(volume, ((1, 1), (0, 0), (0, 0)))
    depth_all = volume.shape[0]

    def march(carry, index):
        color, optical = carry
        slabs = lax.dynamic_slice_in_dim(padded, index, 3, 0)
        cell = slabs[1]
        shade = shading(slabs[0], cell, slabs[2], light)
        ext, emit = classify(cell, tf_center, tf_width, tf_density, tf_color)
        weight = jnp.exp(-optical) * (1.0 - jnp.exp(-ext)) * shade
        return ((color + weight[None] * emit, optical + ext), None)
    start = (jnp.zeros((3,) + volume.shape[1:], jnp.float32), jnp.zeros(volume.shape[1:], jnp.float32))
    (color, optical), unused = lax.scan(march, start, jnp.arange(depth_all, dtype=jnp.int32))
    return jnp.concatenate([color, (1.0 - jnp.exp(-optical))[None]], axis=0)
```

```python
import functools
import math

import jax
import jax.numpy as jnp
from jax import lax
from jax.experimental import pallas as pl
from jax.experimental.pallas import tpu as pltpu
from jax.sharding import PartitionSpec as P

LANES = 128
SUB = 8


def march_kernel(par, vol, low, high, left, right, out, cells, sems):
    depth, rows, cols = vol.shape
    tiles = cols // LANES
    bumps = 8
    copies = []
    for t in range(tiles):
        lanes = pl.ds(t * LANES, LANES)
        for i, (src, dst) in enumerate((
            (vol.at[:, :, lanes], cells.at[t, pl.ds(1, depth), pl.ds(SUB, rows)]),
            (low.at[:, :, lanes], cells.at[t, pl.ds(0, 1), pl.ds(SUB, rows)]),
            (high.at[:, :, lanes], cells.at[t, pl.ds(depth + 1, 1), pl.ds(SUB, rows)]),
        )):
            copies.append(pltpu.make_async_copy(src, dst, sems.at[3 * t + i]))
    for copy in copies:
        copy.start()
    edge = jnp.zeros((tiles, depth + 2, SUB, LANES), jnp.float32)
    cells[:, :, pl.ds(0, SUB), :] = edge
    cells[:, :, pl.ds(SUB + rows, SUB), :] = edge
    for copy in copies:
        copy.wait()

    lane = lax.broadcasted_iota(jnp.int32, (SUB, LANES), 1)
    first = lane == 0
    last = lane == LANES - 1

    def block(rb, unused):
        base = pl.multiple_of(rb * SUB, SUB)

        def cell(t, z, shift=0):
            return cells[t, z, pl.ds(base + SUB + shift, SUB), :]

        halo_left = left[rb]
        halo_right = right[rb]
        acc = [[None] * bumps for t in range(tiles)]
        logt = [None] * tiles
        trans = [None] * tiles
        for z in range(depth):
            here = [cell(t, z + 1) for t in range(tiles)]
            fwd = [pltpu.roll(h, 1, 1) for h in here]
            bwd = [pltpu.roll(h, LANES - 1, 1) for h in here]
            lo = halo_left if z == 0 else pltpu.roll(halo_left, LANES - z, 1)
            hi = pltpu.roll(halo_right, LANES - 1 - z, 1)
            for t in range(tiles):
                v = here[t]
                from_left = jnp.where(first, lo if t == 0 else fwd[t - 1], fwd[t])
                from_right = jnp.where(last, hi if t == tiles - 1 else bwd[t + 1], bwd[t])
                dx = from_right - from_left
                dy = cell(t, z + 1, 1) - cell(t, z + 1, -1)
                dz = cell(t, z + 2) - cell(t, z)
                lit = jnp.abs(par[24] * dx + par[25] * dy + par[26] * dz)
                norm = (dx * dx + dy * dy) + (dz * dz + 4.0)
                shade = 0.3 + lit * lax.rsqrt(norm)
                b = []
                for k in range(bumps):
                    u = v - par[k]
                    b.append(jnp.exp2(u * u * par[8 + k]))
                e = [b[k] * par[16 + k] for k in range(bumps)]
                ext = ((e[0] + e[1]) + (e[2] + e[3])) + ((e[4] + e[5]) + (e[6] + e[7]))
                logt[t] = ext if z == 0 else logt[t] + ext
                after = jnp.exp2(logt[t])
                weight = ((1.0 if z == 0 else trans[t]) - after) * shade
                trans[t] = after
                for k in range(bumps):
                    term = weight * b[k]
                    acc[t][k] = term if z == 0 else acc[t][k] + term
        for t in range(tiles):
            lanes = pl.ds(t * LANES, LANES)
            for c in range(3):
                total = acc[t][0] * par[32 + c * bumps]
                for k in range(1, bumps):
                    total = total + acc[t][k] * par[32 + c * bumps + k]
                out[rb, c, :, lanes] = total
            out[rb, 3, :, lanes] = logt[t]
        return 0

    lax.fori_loop(0, rows // SUB, block, 0)


def march(par, vol, low, high, left, right):
    depth, rows, cols = vol.shape
    blocks = rows // SUB
    anywhere = pl.BlockSpec(memory_space=pl.ANY)
    return pl.pallas_call(
        march_kernel,
        out_shape=jax.ShapeDtypeStruct((blocks, 4, SUB, cols), jnp.float32),
        in_specs=[pl.BlockSpec(memory_space=pltpu.SMEM)] + [anywhere] * 3
        + [pl.BlockSpec(memory_space=pltpu.VMEM)] * 2,
        out_specs=pl.BlockSpec(memory_space=pltpu.VMEM),
        scratch_shapes=[
            pltpu.VMEM((cols // LANES, depth + 2, rows + 2 * SUB, LANES), jnp.float32),
            pltpu.SemaphoreType.DMA((3 * (cols // LANES),)),
        ],
        compiler_params=pltpu.CompilerParams(vmem_limit_bytes=32 * 1024 * 1024),
        name="march",
    )(par, vol, low, high, left, right)


def merge_kernel(parts, out):
    slabs = parts.shape[0]
    color = [parts[0, c] for c in range(3)]
    logt = parts[0, 3]
    for s in range(1, slabs):
        seen = jnp.exp2(logt)
        color = [color[c] + seen * parts[s, c] for c in range(3)]
        logt = logt + parts[s, 3]
    for c in range(3):
        out[c] = color[c]
    out[3] = 1.0 - jnp.exp2(logt)


def merge(parts):
    slabs, channels, rows, cols = parts.shape
    return pl.pallas_call(
        merge_kernel,
        out_shape=jax.ShapeDtypeStruct((channels, rows, cols), jnp.float32),
        in_specs=[pl.BlockSpec(memory_space=pltpu.VMEM)],
        out_specs=pl.BlockSpec(memory_space=pltpu.VMEM),
        name="merge",
    )(parts)


def edge_lanes(column):
    depth, rows = column.shape
    spread = column.reshape(depth, rows // SUB, SUB).transpose(1, 2, 0)
    return jnp.pad(spread, ((0, 0), (0, 0), (0, LANES - depth)))


def on_device(volume, tf_center, tf_width, tf_density, tf_color, light):
    depth, rows, cols = volume.shape
    slabs = lax.axis_size("depth")
    depth_all = depth * slabs
    up = [(i, i + 1) for i in range(slabs - 1)]
    down = [(j, i) for i, j in up]
    low = lax.ppermute(volume[depth - 1:], "depth", up)
    high = lax.ppermute(volume[:1], "depth", down)
    width = lax.axis_size("col")
    east = [(i, i + 1) for i in range(width - 1)]
    west = [(j, i) for i, j in east]
    left = lax.ppermute(volume[:, :, cols - 1], "col", east)
    right = lax.ppermute(volume[:, :, 0], "col", west)

    log2e = math.log2(math.e)
    par = jnp.concatenate([
        tf_center,
        -log2e / jnp.square(tf_width),
        tf_density * (-log2e / depth_all),
        0.7 * light,
        jnp.zeros((5,), jnp.float32),
        tf_color.reshape(-1),
    ])
    parts = march(par, volume, low, high, edge_lanes(left), edge_lanes(right))
    parts = lax.all_to_all(parts, "depth", 0, 0, tiled=True)
    return merge(parts)


def solution(mesh):
    return jax.shard_map(
        on_device,
        mesh=mesh,
        in_specs=(P("depth", None, "col"), P(), P(), P(), P(), P()),
        out_specs=P(None, "depth", "col"),
        check_vma=False,
    )
```

```python
import functools
import math

import jax
import jax.numpy as jnp
from jax import lax
from jax.experimental import pallas as pl
from jax.experimental.pallas import tpu as pltpu
from jax.sharding import PartitionSpec as P

LANES = 128
SUB = 8
BUMPS = 8
LIMIT = 16 * 1024 * 1024
VMEM = pl.BlockSpec(memory_space=pltpu.VMEM)


def split_depth(slabs):
    zs = 8 if slabs == 32 else max(1, slabs // 2)
    return slabs // zs, zs


def prepare_kernel(
    depth_all, vol, first_slab, last_slab, center, width, density, color, light,
    cells, west, east, par, center_here, width_here, density_here, color_here, light_here, sems,
):
    del first_slab, last_slab
    depth, rows, cols = vol.shape
    tiles = cols // LANES
    copies = [
        pltpu.make_async_copy(
            vol.at[:, :, pl.ds(t * LANES, LANES)], cells.at[t, :, pl.ds(SUB, rows)], sems.at[t]
        )
        for t in range(tiles)
    ]
    small = [
        pltpu.make_async_copy(src, dst, sems.at[tiles + i])
        for i, (src, dst) in enumerate((
            (center, center_here), (width, width_here), (density, density_here),
            (color, color_here), (light, light_here),
        ))
    ]
    for copy in small + copies:
        copy.start()
    log2e = math.log2(math.e)

    def spread(ref, row, k):
        return jnp.broadcast_to(ref[pl.ds(row, 1), pl.ds(k, 1)], (SUB, LANES))

    border = jnp.zeros((tiles, depth, SUB, LANES), jnp.float32)
    cells[:, :, pl.ds(0, SUB), :] = border
    cells[:, :, pl.ds(SUB + rows, SUB), :] = border
    for copy in small:
        copy.wait()
    for k in range(BUMPS):
        scale = spread(width_here, 0, k)
        par[k] = spread(center_here, 0, k)
        par[BUMPS + k] = -log2e / (scale * scale)
        par[2 * BUMPS + k] = spread(density_here, 0, k) * (-log2e / depth_all)
        for c in range(3):
            par[32 + c * BUMPS + k] = spread(color_here, c, k)
    for a in range(3):
        par[24 + a] = spread(light_here, 0, a) * 0.7
    lane = lax.broadcasted_iota(jnp.int32, (SUB, LANES), 1)
    groups = west.shape[0]
    per_group = (rows // SUB) // groups

    def extract(t, source, out):
        def group(g, unused):
            packed = jnp.zeros((SUB, LANES), jnp.float32)
            for r in range(per_group):
                base = pl.multiple_of((g * per_group + r + 1) * SUB, SUB)
                for z in range(depth):
                    place = r * depth + z
                    tile = cells[t, z, pl.ds(base, SUB), :]
                    shift = (place - source) % LANES
                    moved = pltpu.roll(tile, shift, 1) if shift else tile
                    packed = jnp.where(lane == place, moved, packed)
            out[g] = packed
            return 0

        lax.fori_loop(0, groups, group, 0)

    copies[0].wait()
    extract(0, 0, west)
    for copy in copies[1:]:
        copy.wait()
    extract(tiles - 1, LANES - 1, east)


def prepare(depth_all, vol, *small):
    depth, rows, cols = vol.shape
    groups = -(-(rows // SUB) * depth // LANES)
    edge = jax.ShapeDtypeStruct((groups, SUB, LANES), jnp.float32)
    return pl.pallas_call(
        functools.partial(prepare_kernel, depth_all),
        out_shape=(
            jax.ShapeDtypeStruct((cols // LANES, depth, rows + 2 * SUB, LANES), jnp.float32),
            edge,
            edge,
            jax.ShapeDtypeStruct((32 + 3 * BUMPS, SUB, LANES), jnp.float32),
        ),
        in_specs=[pl.BlockSpec(memory_space=pl.ANY)] * 8,
        out_specs=(VMEM, VMEM, VMEM, VMEM),
        scratch_shapes=[pltpu.VMEM(x.shape, jnp.float32) for x in small[-5:]]
        + [pltpu.SemaphoreType.DMA((cols // LANES + 5,))],
        compiler_params=pltpu.CompilerParams(vmem_limit_bytes=LIMIT),
        name="prepare",
    )(vol, *small)


def march_kernel(shifts, ys, zs, par, cells, low, high, left, right, *outs):
    tiles, depth = cells.shape[:2]
    here_z = lax.rem(lax.axis_index("depth"), zs)
    lane = lax.broadcasted_iota(jnp.int32, (SUB, LANES), 1)
    first = lane == 0
    last = lane == LANES - 1
    per_group = LANES // depth

    def block(i, unused):
        which, j = lax.div(i, ys), lax.rem(i, ys)
        shift = shifts[0]
        for q in range(1, len(shifts)):
            shift = jnp.where(which == q, shifts[q], shift)
        rb = j * zs + lax.rem(here_z + shift, zs)
        row = pl.multiple_of(rb * SUB, SUB)
        base = pl.multiple_of(rb * SUB + SUB, SUB)

        def cell(t, z, move=0):
            if z < 0 or z >= depth:
                side = low if z < 0 else high
                return side[pl.ds(row, SUB), pl.ds(t * LANES, LANES)]
            return cells[t, z, pl.ds(base + move, SUB), :]

        group = lax.div(rb, per_group)
        turn = lax.rem(LANES - lax.rem(rb, per_group) * depth, LANES)
        halo_left = pltpu.roll(left[group], turn, 1)
        halo_right = pltpu.roll(right[group], turn, 1)
        acc = [[None] * BUMPS for t in range(tiles)]
        logt = [None] * tiles
        trans = [None] * tiles
        for z in range(depth):
            here = [cell(t, z) for t in range(tiles)]
            fwd = [pltpu.roll(h, 1, 1) for h in here]
            bwd = [pltpu.roll(h, LANES - 1, 1) for h in here]
            lo = halo_left if z == 0 else pltpu.roll(halo_left, LANES - z, 1)
            hi = pltpu.roll(halo_right, LANES - 1 - z, 1)
            for t in range(tiles):
                v = here[t]
                from_left = jnp.where(first, lo if t == 0 else fwd[t - 1], fwd[t])
                from_right = jnp.where(last, hi if t == tiles - 1 else bwd[t + 1], bwd[t])
                dx = from_right - from_left
                dy = cell(t, z, 1) - cell(t, z, -1)
                dz = cell(t, z + 1) - cell(t, z - 1)
                lit = jnp.abs(par[24] * dx + par[25] * dy + par[26] * dz)
                norm = (dx * dx + dy * dy) + (dz * dz + 4.0)
                shade = 0.3 + lit * lax.rsqrt(norm)
                b = []
                for k in range(BUMPS):
                    u = v - par[k]
                    b.append(jnp.exp2(u * u * par[8 + k]))
                e = [b[k] * par[16 + k] for k in range(BUMPS)]
                ext = ((e[0] + e[1]) + (e[2] + e[3])) + ((e[4] + e[5]) + (e[6] + e[7]))
                logt[t] = ext if z == 0 else logt[t] + ext
                after = jnp.exp2(logt[t])
                weight = ((1.0 if z == 0 else trans[t]) - after) * shade
                trans[t] = after
                for k in range(BUMPS):
                    term = weight * b[k]
                    acc[t][k] = term if z == 0 else acc[t][k] + term
        totals = []
        for t in range(tiles):
            for c in range(3):
                total = acc[t][0] * par[32 + c * BUMPS]
                for k in range(1, BUMPS):
                    total = total + acc[t][k] * par[32 + c * BUMPS + k]
                totals.append((t, c, total))
            totals.append((t, 3, logt[t]))
        for q, out in enumerate(outs):
            @pl.when(which == q)
            def store():
                for t, c, total in totals:
                    out[j, c, :, pl.ds(t * LANES, LANES)] = total
        return 0

    lax.fori_loop(0, len(shifts) * ys, block, 0)


def march(shifts, ys, zs, par, cells, low, high, left, right):
    tiles, depth = cells.shape[:2]
    work = len(shifts) * ys * SUB * tiles * LANES * depth
    return pl.pallas_call(
        functools.partial(march_kernel, shifts, ys, zs),
        out_shape=[jax.ShapeDtypeStruct((ys, 4, SUB, tiles * LANES), jnp.float32)] * len(shifts),
        in_specs=[VMEM] * 6,
        out_specs=[VMEM] * len(shifts),
        compiler_params=pltpu.CompilerParams(vmem_limit_bytes=LIMIT),
        cost_estimate=pl.CostEstimate(
            flops=80 * work, bytes_accessed=4 * work, transcendentals=10 * work
        ),
        name="march%d" % shifts[0],
    )(par, cells, low, high, left, right)


def over(parts, here):
    color, logt = [jnp.zeros_like(parts[0][0])] * 3, jnp.zeros_like(parts[0][3])
    back, back_logt = color, logt
    for s in reversed(range(len(parts))):
        turn = here == s
        back = [jnp.where(turn, a, b) for a, b in zip(color, back)]
        back_logt = jnp.where(turn, logt, back_logt)
        color = [jnp.where(turn, 0.0, a) for a in color]
        logt = jnp.where(turn, 0.0, logt)
        seen = jnp.exp2(logt)
        color = [a + seen * parts[s][c] for c, a in enumerate(color)]
        logt = logt + parts[s][3]
    seen = jnp.exp2(logt)
    return [a + seen * b for a, b in zip(color, back)], logt + back_logt


def merge_z_kernel(ys, zs, *refs):
    parts, outs = refs[:zs], refs[zs:]
    me = lax.axis_index("depth")
    y, z = lax.div(me, zs), lax.rem(me, zs)
    for t in range(ys):
        j = lax.rem(y + t, ys)
        color, logt = over([[p[j, c] for c in range(4)] for p in parts], z)
        for c in range(3):
            outs[t][c] = color[c]
        outs[t][3] = logt


def merge_z(ys, zs, parts):
    shape = parts[0].shape[1:]
    return pl.pallas_call(
        functools.partial(merge_z_kernel, ys, zs),
        out_shape=[jax.ShapeDtypeStruct(shape, jnp.float32)] * ys,
        in_specs=[VMEM] * zs,
        out_specs=[VMEM] * ys,
        compiler_params=pltpu.CompilerParams(vmem_limit_bytes=LIMIT),
        name="merge_z",
    )(*parts)


def merge_y_kernel(zs, *refs):
    parts, out = refs[:-1], refs[-1]
    y = lax.div(lax.axis_index("depth"), zs)
    color, logt = over([[p[c] for c in range(4)] for p in parts], y)
    for c in range(3):
        out[c] = color[c]
    out[3] = 1.0 - jnp.exp2(logt)


def merge_y(zs, parts):
    return pl.pallas_call(
        functools.partial(merge_y_kernel, zs),
        out_shape=jax.ShapeDtypeStruct(parts[0].shape, jnp.float32),
        in_specs=[VMEM] * len(parts),
        out_specs=VMEM,
        compiler_params=pltpu.CompilerParams(vmem_limit_bytes=LIMIT),
        name="merge_y",
    )(*parts)


def in_hbm(x):
    return pltpu.with_memory_space_constraint(x, pltpu.HBM)


def on_device(volume, tf_center, tf_width, tf_density, tf_color, light):
    depth, rows, cols = volume.shape
    slabs = lax.axis_size("depth")
    ys, zs = split_depth(slabs)
    depth_all = depth * slabs
    up = [(i, i + 1) for i in range(slabs - 1)]
    down = [(j, i) for i, j in up]
    first_slab, last_slab = volume[0], volume[depth - 1]
    low = lax.ppermute(last_slab, "depth", up)
    high = lax.ppermute(first_slab, "depth", down)
    cells, west_edge, east_edge, par = prepare(
        depth_all, in_hbm(volume), first_slab, last_slab, in_hbm(tf_center[None]),
        in_hbm(tf_width[None]), in_hbm(tf_density[None]), in_hbm(tf_color), in_hbm(light[None]),
    )
    width = lax.axis_size("col")
    east = [(i, i + 1) for i in range(width - 1)]
    west = [(j, i) for i, j in east]
    left = lax.ppermute(east_edge, "col", east)
    right = lax.ppermute(west_edge, "col", west)

    order = sorted(range(zs), key=lambda s: -min(s, zs - s))
    arrived = [None] * zs
    cuts = [0, 1, 3, 5, 8] if zs == 8 else [0, zs]
    for begin, end in zip(cuts, cuts[1:]):
        shifts = order[begin:end]
        parts = march(shifts, ys, zs, par, cells, low, high, left, right)
        for s, part in zip(shifts, parts):
            if s:
                pairs = [(y * zs + z, y * zs + (z + s) % zs) for y in range(ys) for z in range(zs)]
                part = lax.ppermute(part, "depth", pairs)
            arrived[s] = part
    merged = list(merge_z(ys, zs, arrived))
    for t in range(1, ys):
        pairs = [(i, (i + t * zs) % slabs) for i in range(slabs)]
        merged[t] = lax.ppermute(merged[t], "depth", pairs)
    return merge_y(zs, merged)


def solution(mesh):
    return jax.shard_map(
        on_device,
        mesh=mesh,
        in_specs=(P("depth", None, "col"), P(), P(), P(), P(), P()),
        out_specs=P(None, "depth", "col"),
        check_vma=False,
    )
```

```python
import functools
import math

import jax
import jax.numpy as jnp
from jax import lax
from jax.experimental import pallas as pl
from jax.experimental.pallas import tpu as pltpu
from jax.sharding import PartitionSpec as P

LANES = 128
SUB = 8
BUMPS = 8
LIMIT = 16 * 1024 * 1024
MIX = 256
BODY = 2
VMEM = pl.BlockSpec(memory_space=pltpu.VMEM)


def split_depth(slabs):
    zs = 8 if slabs == 32 else max(1, slabs // 2)
    return slabs // zs, zs


def thirds(x):
    one = x.astype(jnp.bfloat16).astype(jnp.float32)
    rest = x - one
    two = rest.astype(jnp.bfloat16).astype(jnp.float32)
    return one, two, rest - two


def prepare_kernel(
    depth_all, vol, first_slab, last_slab, center, width, density, color, light,
    cells, west, east, par, mix, center_here, width_here, density_here, color_here, light_here, sems,
):
    del first_slab, last_slab
    depth, rows, cols = vol.shape
    tiles = cols // LANES
    copies = [
        pltpu.make_async_copy(
            vol.at[:, :, pl.ds(t * LANES, LANES)], cells.at[t, :, pl.ds(SUB, rows)], sems.at[t]
        )
        for t in range(tiles)
    ]
    small = [
        pltpu.make_async_copy(src, dst, sems.at[tiles + i])
        for i, (src, dst) in enumerate((
            (center, center_here), (width, width_here), (density, density_here),
            (color, color_here), (light, light_here),
        ))
    ]
    for copy in small + copies:
        copy.start()
    log2e = math.log2(math.e)

    def spread(ref, row, k, lanes=LANES):
        return jnp.broadcast_to(ref[pl.ds(row, 1), pl.ds(k, 1)], (SUB, lanes))

    border = jnp.zeros((tiles, depth, SUB, LANES), jnp.float32)
    cells[:, :, pl.ds(0, SUB), :] = border
    cells[:, :, pl.ds(SUB + rows, SUB), :] = border
    for copy in small:
        copy.wait()
    wide = lax.broadcasted_iota(jnp.int32, (SUB, MIX), 1)
    row = lax.broadcasted_iota(jnp.int32, (SUB, MIX), 0)
    piece, pair, column = wide // 16, (wide // SUB) % 2, wide % SUB
    groups_of = [[], []]
    for k in range(BUMPS):
        scale = spread(width_here, 0, k, MIX)
        middle = spread(center_here, 0, k, MIX)
        dense = spread(density_here, 0, k, MIX) * (log2e / depth_all)
        a = -log2e / (scale * scale)
        parts_a = thirds(a)
        parts_b = thirds(-2.0 * a * middle)
        parts_c = thirds(a * middle * middle + jnp.log(dense) * log2e)
        value = jnp.zeros((SUB, MIX), jnp.float32)
        for first, parts in ((0, parts_a), (6, parts_b)):
            for at, which in enumerate((0, 1, 2, 0, 1, 0)):
                value = jnp.where(piece == first + at, parts[which], value)
        value = jnp.where(column == row, value, 0.0)
        for turn in range(3):
            hit = (piece == 12) & (column == (row + turn) % SUB)
            value = jnp.where(hit, parts_c[turn], value)
        for half in range(2):
            groups_of[half].append(jnp.where(pair == half, value, 0.0))
        dense = dense[:, :LANES]
        for c in range(3):
            par[SUB + c * BUMPS + k] = spread(color_here, c, k) / dense
    for half in range(2):
        for k in range(0, BUMPS, 2):
            both = jnp.concatenate(groups_of[half][k:k + 2], axis=0)
            mix[pl.ds((half * BUMPS + k) * SUB, 2 * SUB), :] = both.astype(jnp.bfloat16)
    for a in range(3):
        par[a] = spread(light_here, 0, a) * 0.7
    lane = lax.broadcasted_iota(jnp.int32, (SUB, LANES), 1)
    groups = west.shape[0]
    per_group = (rows // SUB) // groups

    def extract(t, source, out):
        def group(g, unused):
            packed = jnp.zeros((SUB, LANES), jnp.float32)
            for r in range(per_group):
                base = pl.multiple_of((g * per_group + r + 1) * SUB, SUB)
                for z in range(depth):
                    place = r * depth + z
                    tile = cells[t, z, pl.ds(base, SUB), :]
                    shift = (place - source) % LANES
                    moved = pltpu.roll(tile, shift, 1) if shift else tile
                    packed = jnp.where(lane == place, moved, packed)
            out[g] = packed
            return 0

        lax.fori_loop(0, groups, group, 0)

    copies[0].wait()
    extract(0, 0, west)
    for copy in copies[1:]:
        copy.wait()
    extract(tiles - 1, LANES - 1, east)


def prepare(depth_all, vol, *small):
    depth, rows, cols = vol.shape
    groups = -(-(rows // SUB) * depth // LANES)
    edge = jax.ShapeDtypeStruct((groups, SUB, LANES), jnp.float32)
    return pl.pallas_call(
        functools.partial(prepare_kernel, depth_all),
        out_shape=(
            jax.ShapeDtypeStruct((cols // LANES, depth, rows + 2 * SUB, LANES), jnp.float32),
            edge,
            edge,
            jax.ShapeDtypeStruct((SUB + 3 * BUMPS, SUB, LANES), jnp.float32),
            jax.ShapeDtypeStruct((2 * BUMPS * SUB, MIX), jnp.bfloat16),
        ),
        in_specs=[pl.BlockSpec(memory_space=pl.ANY)] * 8,
        out_specs=(VMEM,) * 5,
        scratch_shapes=[pltpu.VMEM(x.shape, jnp.float32) for x in small[-5:]]
        + [pltpu.SemaphoreType.DMA((cols // LANES + 5,))],
        compiler_params=pltpu.CompilerParams(vmem_limit_bytes=LIMIT),
        name="prepare",
    )(vol, *small)


def split(x):
    one = x.astype(jnp.bfloat16)
    rest = x - one.astype(jnp.float32)
    two = rest.astype(jnp.bfloat16)
    return one, two, (rest - two.astype(jnp.float32)).astype(jnp.bfloat16)


def march_kernel(away, extra, near, ys, zs, par, mix, cells, low, high, left, right, *refs):
    tiles, depth = cells.shape[:2]
    slab, column = lax.axis_index("depth"), lax.axis_index("col")
    here_z = lax.rem(slab, zs)
    has_low, has_high = slab > 0, slab < lax.axis_size("depth") - 1
    has_left, has_right = column > 0, column < lax.axis_size("col") - 1
    lane = lax.broadcasted_iota(jnp.int32, (SUB, LANES), 1)
    first = lane == 0
    last = lane == LANES - 1
    per_group = LANES // depth
    odd = lax.rem(here_z, 2)
    side = 2 * odd - 1
    origin, sign = (here_z - side, -side) if away else (here_z, side)
    targets = [lax.rem(origin + sign * d + zs, zs) for d in near]
    other, outs = (None, refs[extra:]) if away else (refs[0], refs[1 + extra:])
    ones = jnp.ones((2 * SUB, tiles * LANES), jnp.bfloat16)
    zeros = jnp.zeros((2 * SUB, tiles * LANES), jnp.bfloat16)

    def exponents(rb, p):
        base = pl.multiple_of(rb * SUB + SUB, SUB)
        pair = jnp.concatenate([
            jnp.concatenate(
                [cells[t, 2 * p + h, pl.ds(base, SUB), :] for t in range(tiles)], axis=1
            )
            for h in range(2)
        ], axis=0)
        v1, v2, v3 = split(pair)
        q1, q2, q3 = split(pair * pair)
        return jnp.dot(
            mix[...],
            jnp.concatenate(
                [q1, q1, q1, q2, q2, q3, v1, v1, v1, v2, v2, v3, ones, zeros, zeros, zeros], axis=0
            ),
            preferred_element_type=jnp.float32,
        )

    def block(rb):
        row = pl.multiple_of(rb * SUB, SUB)
        base = pl.multiple_of(rb * SUB + SUB, SUB)

        def cell(t, z, move=0):
            if z < 0 or z >= depth:
                beyond, inside = (low, has_low) if z < 0 else (high, has_high)
                return jnp.where(inside, beyond[pl.ds(row, SUB), pl.ds(t * LANES, LANES)], 0.0)
            return cells[t, z, pl.ds(base + move, SUB), :]

        group = lax.div(rb, per_group)
        turn = lax.rem(LANES - lax.rem(rb, per_group) * depth, LANES)
        halo_left = pltpu.roll(jnp.where(has_left, left[group], 0.0), turn, 1)
        halo_right = pltpu.roll(jnp.where(has_right, right[group], 0.0), turn, 1)
        acc = [[None] * BUMPS for t in range(tiles)]
        logt = [None] * tiles
        trans = [None] * tiles
        for z in range(depth):
            if z % 2 == 0:
                power = exponents(rb, z // 2)
            here = [cell(t, z) for t in range(tiles)]
            fwd = [pltpu.roll(h, 1, 1) for h in here]
            bwd = [pltpu.roll(h, LANES - 1, 1) for h in here]
            lo = halo_left if z == 0 else pltpu.roll(halo_left, LANES - z, 1)
            hi = pltpu.roll(halo_right, LANES - 1 - z, 1)
            for t in range(tiles):
                from_left = jnp.where(first, lo if t == 0 else fwd[t - 1], fwd[t])
                from_right = jnp.where(last, hi if t == tiles - 1 else bwd[t + 1], bwd[t])
                dx = from_right - from_left
                dy = cell(t, z, 1) - cell(t, z, -1)
                dz = cell(t, z + 1) - cell(t, z - 1)
                lit = jnp.abs(par[0] * dx + par[1] * dy + par[2] * dz)
                norm = (dx * dx + dy * dy) + (dz * dz + 4.0)
                shade = 0.3 + lit * lax.rsqrt(norm)
                lanes = slice(t * LANES, (t + 1) * LANES)
                top = (z % 2) * BUMPS * SUB
                b = [
                    jnp.exp2(power[top + k * SUB:top + (k + 1) * SUB, lanes])
                    for k in range(BUMPS)
                ]
                ext = ((b[0] + b[1]) + (b[2] + b[3])) + ((b[4] + b[5]) + (b[6] + b[7]))
                logt[t] = -ext if z == 0 else logt[t] - ext
                after = jnp.exp2(logt[t])
                weight = ((1.0 if z == 0 else trans[t]) - after) * shade
                trans[t] = after
                for k in range(BUMPS):
                    term = weight * b[k]
                    acc[t][k] = term if z == 0 else acc[t][k] + term
        totals = [[] for t in range(tiles)]
        for t in range(tiles):
            for c in range(3):
                total = acc[t][0] * par[SUB + c * BUMPS]
                for k in range(1, BUMPS):
                    total = total + acc[t][k] * par[SUB + c * BUMPS + k]
                totals[t].append(total)
            totals[t].append(logt[t])
        return totals

    unroll = max(1, min(ys, BODY // len(near)))

    def step(i, unused):
        for u in range(unroll):
            j = i * unroll + u
            for q in range(len(near)):
                for t, totals in enumerate(block(j * zs + targets[q])):
                    lanes = pl.ds(t * LANES, LANES)
                    if away:
                        for c in range(4):
                            outs[0][q, j, c, :, lanes] = totals[c]
                    else:
                        mate = [other[q, j, c, :, lanes] for c in range(4)]
                        ahead = [jnp.where(odd == 1, m, a) for a, m in zip(totals, mate)]
                        behind = [jnp.where(odd == 1, a, m) for a, m in zip(totals, mate)]
                        seen = jnp.exp2(ahead[3])
                        for c in range(3):
                            outs[q][j, c, :, lanes] = ahead[c] + seen * behind[c]
                        outs[q][j, 3, :, lanes] = ahead[3] + behind[3]
        return 0

    lax.fori_loop(0, ys // unroll, step, 0)


def march(name, near, ys, zs, par, mix, cells, low, high, left, right, other=None, after=()):
    tiles, depth = cells.shape[:2]
    away = other is None
    work = len(near) * ys * SUB * tiles * LANES * depth
    one = (ys, 4, SUB, tiles * LANES)
    if away:
        shapes = [jax.ShapeDtypeStruct((len(near),) + one, jnp.float32)]
    else:
        shapes = [jax.ShapeDtypeStruct(one, jnp.float32)] * len(near)
    operands = (par, mix, cells, low, high, left, right) + (() if away else (other,))
    return pl.pallas_call(
        functools.partial(march_kernel, away, len(after), near, ys, zs),
        out_shape=shapes,
        in_specs=[VMEM] * len(operands) + [pl.BlockSpec(memory_space=pl.ANY)] * len(after),
        out_specs=[VMEM] * len(shapes),
        compiler_params=pltpu.CompilerParams(vmem_limit_bytes=LIMIT),
        cost_estimate=pl.CostEstimate(
            flops=80 * work, bytes_accessed=4 * work, transcendentals=10 * work
        ),
        name=name,
    )(*operands, *after)


def over(parts, here):
    color, logt = [jnp.zeros_like(parts[0][0])] * 3, jnp.zeros_like(parts[0][3])
    back, back_logt = color, logt
    for s in reversed(range(len(parts))):
        turn = here == s
        back = [jnp.where(turn, a, b) for a, b in zip(color, back)]
        back_logt = jnp.where(turn, logt, back_logt)
        color = [jnp.where(turn, 0.0, a) for a in color]
        logt = jnp.where(turn, 0.0, logt)
        seen = jnp.exp2(logt)
        color = [a + seen * parts[s][c] for c, a in enumerate(color)]
        logt = logt + parts[s][3]
    seen = jnp.exp2(logt)
    return [a + seen * b for a, b in zip(color, back)], logt + back_logt


def hold(parts, work):
    anywhere = [pl.BlockSpec(memory_space=pl.ANY)] * len(parts)
    return pl.pallas_call(
        lambda *refs: None,
        out_shape=[jax.ShapeDtypeStruct(p.shape, p.dtype) for p in parts],
        in_specs=anywhere,
        out_specs=anywhere,
        input_output_aliases={i: i for i in range(len(parts))},
        compiler_params=pltpu.CompilerParams(vmem_limit_bytes=LIMIT),
        cost_estimate=pl.CostEstimate(flops=80 * work, bytes_accessed=4 * work, transcendentals=10 * work),
        name="hold",
    )(*parts)


def merge_z_kernel(ys, zs, *refs):
    pairs = len(refs) - ys
    parts, outs = refs[:pairs], refs[pairs:]
    me = lax.axis_index("depth")
    y, z = lax.div(me, zs), lax.rem(me, zs)
    odd = lax.rem(z, 2) == 1
    for t in range(ys):
        j = lax.rem(y + t, ys)
        held = [[p[j, c] for c in range(4)] for p in parts]
        ring = [held[0]] + [None] * (pairs - 1)
        for r in range(1, pairs):
            even_from = 2 * r - 1 if 2 * r <= pairs else 2 * (pairs - r)
            odd_from = 2 * r if 2 * r < pairs else 2 * (pairs - r) - 1
            ring[r] = [
                jnp.where(odd, a, b) for a, b in zip(held[odd_from], held[even_from])
            ]
        color, logt = over(ring, lax.div(z, 2))
        for c in range(3):
            outs[t][c] = color[c]
        outs[t][3] = logt


def merge_z(ys, zs, parts):
    shape = parts[0].shape[1:]
    return pl.pallas_call(
        functools.partial(merge_z_kernel, ys, zs),
        out_shape=[jax.ShapeDtypeStruct(shape, jnp.float32)] * ys,
        in_specs=[VMEM] * len(parts),
        out_specs=[VMEM] * ys,
        compiler_params=pltpu.CompilerParams(vmem_limit_bytes=LIMIT),
        name="merge_z",
    )(*parts)


def merge_y_kernel(zs, *refs):
    parts, out = refs[:-1], refs[-1]
    y = lax.div(lax.axis_index("depth"), zs)
    color, logt = over([[p[c] for c in range(4)] for p in parts], y)
    for c in range(3):
        out[c] = color[c]
    out[3] = 1.0 - jnp.exp2(logt)


def merge_y(zs, parts):
    return pl.pallas_call(
        functools.partial(merge_y_kernel, zs),
        out_shape=jax.ShapeDtypeStruct(parts[0].shape, jnp.float32),
        in_specs=[VMEM] * len(parts),
        out_specs=VMEM,
        compiler_params=pltpu.CompilerParams(vmem_limit_bytes=LIMIT),
        name="merge_y",
    )(*parts)


def in_hbm(x):
    return pltpu.with_memory_space_constraint(x, pltpu.HBM)


def on_device(volume, tf_center, tf_width, tf_density, tf_color, light):
    depth, rows, cols = volume.shape
    slabs = lax.axis_size("depth")
    ys, zs = split_depth(slabs)
    depth_all = depth * slabs
    up = [(i, (i + 1) % slabs) for i in range(slabs)]
    down = [(j, i) for i, j in up]
    first_slab, last_slab = volume[0], volume[depth - 1]
    low = lax.ppermute(last_slab, "depth", up)
    high = lax.ppermute(first_slab, "depth", down)
    cells, west_edge, east_edge, par, mix = prepare(
        depth_all, in_hbm(volume), first_slab, last_slab, in_hbm(tf_center[None]),
        in_hbm(tf_width[None]), in_hbm(tf_density[None]), in_hbm(tf_color), in_hbm(light[None]),
    )
    width = lax.axis_size("col")
    east = [(i, (i + 1) % width) for i in range(width)]
    west = [(j, i) for i, j in east]
    left = lax.ppermute(east_edge, "col", east)
    right = lax.ppermute(west_edge, "col", west)

    def along_z(x, to):
        return lax.ppermute(
            x, "depth", [(y * zs + z, y * zs + to(z) % zs) for y in range(ys) for z in range(zs)]
        )

    common = (ys, zs, par, mix, cells, low, high, left, right)
    reach = (zs - 2) // 2
    far = list(range(reach, 0, -1)) + [0]
    stages = [far[:2], far[2:]] if len(far) > 2 else [far]
    given, after = [], ()
    for i, near in enumerate(stages):
        parts = march("away%d" % i, near, *common, after=after)[0]
        given.append(along_z(parts, lambda z: z ^ 1))
        after = (parts,)
    arrived = [None] * (reach + 1)
    for i, near in enumerate(stages):
        parts = march("keep%d" % i, near, *common, other=given[i], after=after)
        for d, part in zip(near, parts):
            arrived[d] = along_z(part, lambda z: z + d if z % 2 else z - d) if d else part
        after = (parts[0],)
    early = [d for d in stages[0] if d] if len(stages) > 1 else []
    for d, part in zip(early, hold([arrived[d] for d in early], 16 * arrived[0].size) if early else []):
        arrived[d] = part
    merged = list(merge_z(ys, zs, arrived))
    for t in range(1, ys):
        pairs = [(i, (i + t * zs) % slabs) for i in range(slabs)]
        merged[t] = lax.ppermute(merged[t], "depth", pairs)
    return merge_y(zs, merged)


def solution(mesh):
    return jax.shard_map(
        on_device,
        mesh=mesh,
        in_specs=(P("depth", None, "col"), P(), P(), P(), P(), P()),
        out_specs=P(None, "depth", "col"),
        check_vma=False,
    )
```

```python
import functools
import math

import jax
import jax.numpy as jnp
from jax import lax
from jax.experimental import pallas as pl
from jax.experimental.pallas import tpu as pltpu
from jax.sharding import PartitionSpec as P

LANES = 128
SUB = 8
BUMPS = 8
LIMIT = 16 * 1024 * 1024
MIX = 256
BODY = 2
VMEM = pl.BlockSpec(memory_space=pltpu.VMEM)


def split_depth(slabs):
    zs = 8 if slabs == 32 else max(1, slabs // 2)
    return slabs // zs, zs


def thirds(x):
    one = x.astype(jnp.bfloat16).astype(jnp.float32)
    rest = x - one
    two = rest.astype(jnp.bfloat16).astype(jnp.float32)
    return one, two, rest - two


def prepare_kernel(
    depth_all, vol, first_slab, last_slab, center, width, density, color, light,
    cells, west, east, par, mix, center_here, width_here, density_here, color_here, light_here, sems,
):
    del first_slab, last_slab
    depth, rows, cols = vol.shape
    tiles = cols // LANES
    groups = west.shape[0]
    band = rows // groups

    def load(t, g):
        return pltpu.make_async_copy(
            vol.at[:, pl.ds(g * band, band), pl.ds(t * LANES, LANES)],
            cells.at[t, :, pl.ds(SUB + g * band, band)],
            sems.at[t * groups + g],
        )

    edges = list(dict.fromkeys((0, tiles - 1)))
    order = edges + [t for t in range(tiles) if t not in edges]
    copies = [load(t, g) for g in range(groups) for t in order]
    small = [
        pltpu.make_async_copy(src, dst, sems.at[tiles * groups + i])
        for i, (src, dst) in enumerate((
            (center, center_here), (width, width_here), (density, density_here),
            (color, color_here), (light, light_here),
        ))
    ]
    for copy in small + copies:
        copy.start()
    log2e = math.log2(math.e)

    def spread(ref, row, k, lanes=LANES):
        return jnp.broadcast_to(ref[pl.ds(row, 1), pl.ds(k, 1)], (SUB, lanes))

    border = jnp.zeros((tiles, depth, SUB, LANES), jnp.float32)
    cells[:, :, pl.ds(0, SUB), :] = border
    cells[:, :, pl.ds(SUB + rows, SUB), :] = border
    for copy in small:
        copy.wait()
    wide = lax.broadcasted_iota(jnp.int32, (SUB, MIX), 1)
    row = lax.broadcasted_iota(jnp.int32, (SUB, MIX), 0)
    piece, pair, column = wide // 16, (wide // SUB) % 2, wide % SUB
    groups_of = [[], []]
    for k in range(BUMPS):
        scale = spread(width_here, 0, k, MIX)
        middle = spread(center_here, 0, k, MIX)
        dense = spread(density_here, 0, k, MIX) * (log2e / depth_all)
        a = -log2e / (scale * scale)
        parts_a = thirds(a)
        parts_b = thirds(-2.0 * a * middle)
        parts_c = thirds(a * middle * middle + jnp.log(dense) * log2e)
        value = jnp.zeros((SUB, MIX), jnp.float32)
        for first, parts in ((0, parts_a), (6, parts_b)):
            for at, which in enumerate((0, 1, 2, 0, 1, 0)):
                value = jnp.where(piece == first + at, parts[which], value)
        value = jnp.where(column == row, value, 0.0)
        for turn in range(3):
            hit = (piece == 12) & (column == (row + turn) % SUB)
            value = jnp.where(hit, parts_c[turn], value)
        for half in range(2):
            groups_of[half].append(jnp.where(pair == half, value, 0.0))
        dense = dense[:, :LANES]
        for c in range(3):
            par[SUB + c * BUMPS + k] = spread(color_here, c, k) / dense
    for half in range(2):
        for k in range(0, BUMPS, 2):
            both = jnp.concatenate(groups_of[half][k:k + 2], axis=0)
            mix[pl.ds((half * BUMPS + k) * SUB, 2 * SUB), :] = both.astype(jnp.bfloat16)
    for a in range(3):
        par[a] = spread(light_here, 0, a) * 0.7
    lane = lax.broadcasted_iota(jnp.int32, (SUB, LANES), 1)
    per_group = band // SUB

    def extract(t, g, source, out):
        packed = jnp.zeros((SUB, LANES), jnp.float32)
        for r in range(per_group):
            for z in range(depth):
                place = r * depth + z
                tile = cells[t, z, pl.ds((g * per_group + r + 1) * SUB, SUB), :]
                shift = (place - source) % LANES
                moved = pltpu.roll(tile, shift, 1) if shift else tile
                packed = jnp.where(lane == place, moved, packed)
        out[g] = packed

    waits = iter(copies)
    for g in range(groups):
        for t in order:
            next(waits).wait()
        extract(0, g, 0, west)
        extract(tiles - 1, g, LANES - 1, east)


def prepare(depth_all, vol, *small):
    depth, rows, cols = vol.shape
    groups = -(-(rows // SUB) * depth // LANES)
    edge = jax.ShapeDtypeStruct((groups, SUB, LANES), jnp.float32)
    return pl.pallas_call(
        functools.partial(prepare_kernel, depth_all),
        out_shape=(
            jax.ShapeDtypeStruct((cols // LANES, depth, rows + 2 * SUB, LANES), jnp.float32),
            edge,
            edge,
            jax.ShapeDtypeStruct((SUB + 3 * BUMPS, SUB, LANES), jnp.float32),
            jax.ShapeDtypeStruct((2 * BUMPS * SUB, MIX), jnp.bfloat16),
        ),
        in_specs=[pl.BlockSpec(memory_space=pl.ANY)] * 8,
        out_specs=(VMEM,) * 5,
        scratch_shapes=[pltpu.VMEM(x.shape, jnp.float32) for x in small[-5:]]
        + [pltpu.SemaphoreType.DMA((cols // LANES * groups + 5,))],
        compiler_params=pltpu.CompilerParams(vmem_limit_bytes=LIMIT),
        name="prepare",
    )(vol, *small)


def split(x):
    one = x.astype(jnp.bfloat16)
    rest = x - one.astype(jnp.float32)
    two = rest.astype(jnp.bfloat16)
    return one, two, (rest - two.astype(jnp.float32)).astype(jnp.bfloat16)


def march_kernel(away, slot, extra, near, ys, zs, par, mix, cells, low, high, left, right, *refs):
    tiles, depth = cells.shape[:2]
    slab, column = lax.axis_index("depth"), lax.axis_index("col")
    here_z = lax.rem(slab, zs)
    has_low, has_high = slab > 0, slab < lax.axis_size("depth") - 1
    has_left, has_right = column > 0, column < lax.axis_size("col") - 1
    lane = lax.broadcasted_iota(jnp.int32, (SUB, LANES), 1)
    first = lane == 0
    last = lane == LANES - 1
    per_group = LANES // depth
    odd = lax.rem(here_z, 2)
    side = 2 * odd - 1
    origin, sign = (here_z - side, -side) if away else (here_z, side)
    targets = [lax.rem(origin + sign * d + zs, zs) for d in near]
    other, outs = (None, refs[extra:]) if slot is None else (refs[0], refs[1 + extra:])
    ones = jnp.ones((2 * SUB, tiles * LANES), jnp.bfloat16)
    zeros = jnp.zeros((2 * SUB, tiles * LANES), jnp.bfloat16)

    def exponents(rb, p):
        base = pl.multiple_of(rb * SUB + SUB, SUB)
        pair = jnp.concatenate([
            jnp.concatenate(
                [cells[t, 2 * p + h, pl.ds(base, SUB), :] for t in range(tiles)], axis=1
            )
            for h in range(2)
        ], axis=0)
        v1, v2, v3 = split(pair)
        q1, q2, q3 = split(pair * pair)
        return jnp.dot(
            mix[...],
            jnp.concatenate(
                [q1, q1, q1, q2, q2, q3, v1, v1, v1, v2, v2, v3, ones, zeros, zeros, zeros], axis=0
            ),
            preferred_element_type=jnp.float32,
        )

    def block(rb):
        row = pl.multiple_of(rb * SUB, SUB)
        base = pl.multiple_of(rb * SUB + SUB, SUB)

        def cell(t, z, move=0):
            if z < 0 or z >= depth:
                beyond, inside = (low, has_low) if z < 0 else (high, has_high)
                return jnp.where(inside, beyond[pl.ds(row, SUB), pl.ds(t * LANES, LANES)], 0.0)
            return cells[t, z, pl.ds(base + move, SUB), :]

        group = lax.div(rb, per_group)
        turn = lax.rem(LANES - lax.rem(rb, per_group) * depth, LANES)
        halo_left = pltpu.roll(jnp.where(has_left, left[group], 0.0), turn, 1)
        halo_right = pltpu.roll(jnp.where(has_right, right[group], 0.0), turn, 1)
        acc = [[None] * BUMPS for t in range(tiles)]
        logt = [None] * tiles
        trans = [None] * tiles
        for z in range(depth):
            if z % 2 == 0:
                power = exponents(rb, z // 2)
            here = [cell(t, z) for t in range(tiles)]
            fwd = [pltpu.roll(h, 1, 1) for h in here]
            bwd = [pltpu.roll(h, LANES - 1, 1) for h in here]
            lo = halo_left if z == 0 else pltpu.roll(halo_left, LANES - z, 1)
            hi = pltpu.roll(halo_right, LANES - 1 - z, 1)
            for t in range(tiles):
                from_left = jnp.where(first, lo if t == 0 else fwd[t - 1], fwd[t])
                from_right = jnp.where(last, hi if t == tiles - 1 else bwd[t + 1], bwd[t])
                dx = from_right - from_left
                dy = cell(t, z, 1) - cell(t, z, -1)
                dz = cell(t, z + 1) - cell(t, z - 1)
                lit = jnp.abs(par[0] * dx + par[1] * dy + par[2] * dz)
                norm = (dx * dx + dy * dy) + (dz * dz + 4.0)
                shade = 0.3 + lit * lax.rsqrt(norm)
                lanes = slice(t * LANES, (t + 1) * LANES)
                top = (z % 2) * BUMPS * SUB
                b = [
                    jnp.exp2(power[top + k * SUB:top + (k + 1) * SUB, lanes])
                    for k in range(BUMPS)
                ]
                ext = ((b[0] + b[1]) + (b[2] + b[3])) + ((b[4] + b[5]) + (b[6] + b[7]))
                logt[t] = -ext if z == 0 else logt[t] - ext
                after = jnp.exp2(logt[t])
                weight = ((1.0 if z == 0 else trans[t]) - after) * shade
                trans[t] = after
                for k in range(BUMPS):
                    term = weight * b[k]
                    acc[t][k] = term if z == 0 else acc[t][k] + term
        totals = [[] for t in range(tiles)]
        for t in range(tiles):
            for c in range(3):
                total = acc[t][0] * par[SUB + c * BUMPS]
                for k in range(1, BUMPS):
                    total = total + acc[t][k] * par[SUB + c * BUMPS + k]
                totals[t].append(total)
            totals[t].append(logt[t])
        return totals

    unroll = max(1, min(ys, BODY // len(near)))

    def step(i, unused):
        for u in range(unroll):
            j = i * unroll + u
            for q in range(len(near)):
                for t, totals in enumerate(block(j * zs + targets[q])):
                    lanes = pl.ds(t * LANES, LANES)
                    if other is not None:
                        mate = [other[slot + q, j, c, :, lanes] for c in range(4)]
                        totals = pair_over(totals, mate, odd == 1)
                    for c in range(4):
                        outs[0][q, j, c, :, lanes] = totals[c]
        return 0

    lax.fori_loop(0, ys // unroll, step, 0)


def march(name, away, near, ys, zs, par, mix, cells, low, high, left, right, other=None, after=()):
    tiles, depth = cells.shape[:2]
    work = len(near) * ys * SUB * tiles * LANES * depth
    shape = (len(near), ys, 4, SUB, tiles * LANES)
    mate, slot = ((), None) if other is None else ((other[0],), other[1])
    operands = (par, mix, cells, low, high, left, right) + mate
    return pl.pallas_call(
        functools.partial(march_kernel, away, slot, len(after), near, ys, zs),
        out_shape=jax.ShapeDtypeStruct(shape, jnp.float32),
        in_specs=[VMEM] * len(operands) + [pl.BlockSpec(memory_space=pl.ANY)] * len(after),
        out_specs=VMEM,
        compiler_params=pltpu.CompilerParams(vmem_limit_bytes=LIMIT),
        cost_estimate=pl.CostEstimate(
            flops=80 * work, bytes_accessed=4 * work, transcendentals=10 * work
        ),
        name=name,
    )(*operands, *after)


def pair_over(own, mate, mate_nearer):
    ahead = [jnp.where(mate_nearer, m, a) for a, m in zip(own, mate)]
    behind = [jnp.where(mate_nearer, a, m) for a, m in zip(own, mate)]
    seen = jnp.exp2(ahead[3])
    return [a + seen * b for a, b in zip(ahead[:3], behind[:3])] + [ahead[3] + behind[3]]


def over(parts, here):
    color, logt = [jnp.zeros_like(parts[0][0])] * 3, jnp.zeros_like(parts[0][3])
    back, back_logt = color, logt
    for s in reversed(range(len(parts))):
        turn = here == s
        back = [jnp.where(turn, a, b) for a, b in zip(color, back)]
        back_logt = jnp.where(turn, logt, back_logt)
        color = [jnp.where(turn, 0.0, a) for a in color]
        logt = jnp.where(turn, 0.0, logt)
        seen = jnp.exp2(logt)
        color = [a + seen * parts[s][c] for c, a in enumerate(color)]
        logt = logt + parts[s][3]
    seen = jnp.exp2(logt)
    return [a + seen * b for a, b in zip(color, back)], logt + back_logt


def hold(parts, work):
    anywhere = [pl.BlockSpec(memory_space=pl.ANY)] * len(parts)
    return pl.pallas_call(
        lambda *refs: None,
        out_shape=[jax.ShapeDtypeStruct(p.shape, p.dtype) for p in parts],
        in_specs=anywhere,
        out_specs=anywhere,
        input_output_aliases={i: i for i in range(len(parts))},
        compiler_params=pltpu.CompilerParams(vmem_limit_bytes=LIMIT),
        cost_estimate=pl.CostEstimate(flops=80 * work, bytes_accessed=4 * work, transcendentals=10 * work),
        name="hold",
    )(*parts)


def merge_z_kernel(ys, zs, *refs):
    pairs = zs // 2
    loose = 2 * min(2, pairs)
    singles, parts, outs = refs[:loose], refs[loose:-ys], refs[-ys:]
    me = lax.axis_index("depth")
    y, z = lax.div(me, zs), lax.rem(me, zs)
    odd = lax.rem(z, 2) == 1
    for t in range(ys):
        j = lax.rem(y + t, ys)
        held = [[p[0, j, c] for c in range(4)] for p in singles]
        held = [
            pair_over(held[i], held[i + 1], odd if i == 0 else jnp.logical_not(odd))
            for i in range(0, loose, 2)
        ]
        held += [[p[0, j, c] for c in range(4)] for p in parts]
        ring = [held[0]] + [None] * (pairs - 1)
        for r in range(1, pairs):
            even_from = 2 * r - 1 if 2 * r <= pairs else 2 * (pairs - r)
            odd_from = 2 * r if 2 * r < pairs else 2 * (pairs - r) - 1
            ring[r] = [
                jnp.where(odd, a, b) for a, b in zip(held[odd_from], held[even_from])
            ]
        color, logt = over(ring, lax.div(z, 2))
        for c in range(3):
            outs[t][c] = color[c]
        outs[t][3] = logt


def merge_z(ys, zs, parts):
    shape = parts[0].shape[2:]
    return pl.pallas_call(
        functools.partial(merge_z_kernel, ys, zs),
        out_shape=[jax.ShapeDtypeStruct(shape, jnp.float32)] * ys,
        in_specs=[VMEM] * len(parts),
        out_specs=[VMEM] * ys,
        compiler_params=pltpu.CompilerParams(vmem_limit_bytes=LIMIT),
        name="merge_z",
    )(*parts)


def merge_y_kernel(zs, *refs):
    parts, out = refs[:-1], refs[-1]
    y = lax.div(lax.axis_index("depth"), zs)
    color, logt = over([[p[c] for c in range(4)] for p in parts], y)
    for c in range(3):
        out[c] = color[c]
    out[3] = 1.0 - jnp.exp2(logt)


def merge_y(zs, parts):
    return pl.pallas_call(
        functools.partial(merge_y_kernel, zs),
        out_shape=jax.ShapeDtypeStruct(parts[0].shape, jnp.float32),
        in_specs=[VMEM] * len(parts),
        out_specs=VMEM,
        compiler_params=pltpu.CompilerParams(vmem_limit_bytes=LIMIT),
        name="merge_y",
    )(*parts)


def in_hbm(x):
    return pltpu.with_memory_space_constraint(x, pltpu.HBM)


def on_device(volume, tf_center, tf_width, tf_density, tf_color, light):
    depth, rows, cols = volume.shape
    slabs = lax.axis_size("depth")
    ys, zs = split_depth(slabs)
    depth_all = depth * slabs
    up = [(i, (i + 1) % slabs) for i in range(slabs)]
    down = [(j, i) for i, j in up]
    first_slab, last_slab = volume[0], volume[depth - 1]
    low = lax.ppermute(last_slab, "depth", up)
    high = lax.ppermute(first_slab, "depth", down)
    cells, west_edge, east_edge, par, mix = prepare(
        depth_all, in_hbm(volume), first_slab, last_slab, in_hbm(tf_center[None]),
        in_hbm(tf_width[None]), in_hbm(tf_density[None]), in_hbm(tf_color), in_hbm(light[None]),
    )
    width = lax.axis_size("col")
    east = [(i, (i + 1) % width) for i in range(width)]
    west = [(j, i) for i, j in east]
    left = lax.ppermute(east_edge, "col", east)
    right = lax.ppermute(west_edge, "col", west)

    def along_z(x, to):
        return lax.ppermute(
            x, "depth", [(y * zs + z, y * zs + to(z) % zs) for y in range(ys) for z in range(zs)]
        )

    common = (ys, zs, par, mix, cells, low, high, left, right)
    reach = (zs - 2) // 2
    far = list(range(reach, 1, -1))
    after, incoming = (), {}

    def step(name, away, near, other=None):
        nonlocal after
        parts = march(name, away, near, *common, other=other, after=after)
        after = (parts,)
        return parts

    if far:
        given = along_z(step("away", True, far), lambda z: z ^ 1)
    if reach:
        incoming["near"] = along_z(step("near", False, [1]), lambda z: z + 1 if z % 2 else z - 1)
        incoming["past"] = along_z(step("past", True, [1]), lambda z: z - 2 if z % 2 else z + 2)
    for slot, d in enumerate(far):
        parts = step("keep%d" % d, False, [d], other=(given, slot))
        incoming[d] = along_z(parts, lambda z: z + d if z % 2 else z - d)
    mate = along_z(step("mate", True, [0]), lambda z: z ^ 1)
    own = step("own", False, [0])
    for count in range(1, len(incoming) + 1):
        early = list(incoming)[:count]
        for key, part in zip(early, hold([incoming[key] for key in early], 16 * own.size)):
            incoming[key] = part
    loose = [own, mate] + ([incoming["near"], incoming["past"]] if reach else [])
    merged = list(merge_z(ys, zs, loose + [incoming[d] for d in reversed(far)]))
    for t in range(1, ys):
        pairs = [(i, (i + t * zs) % slabs) for i in range(slabs)]
        merged[t] = lax.ppermute(merged[t], "depth", pairs)
    return merge_y(zs, merged)


def solution(mesh):
    return jax.shard_map(
        on_device,
        mesh=mesh,
        in_specs=(P("depth", None, "col"), P(), P(), P(), P(), P()),
        out_specs=P(None, "depth", "col"),
        check_vma=False,
    )
```

```python
import functools
import math

import jax
import jax.numpy as jnp
from jax import lax
from jax.experimental import pallas as pl
from jax.experimental.pallas import tpu as pltpu
from jax.sharding import PartitionSpec as P

LANES = 128
SUB = 8
BUMPS = 8
LIMIT = 16 * 1024 * 1024
MIX = 256
BODY = 4
VMEM = pl.BlockSpec(memory_space=pltpu.VMEM)


def split_depth(slabs):
    zs = 8 if slabs == 32 else max(1, slabs // 2)
    return slabs // zs, zs


def thirds(x):
    one = x.astype(jnp.bfloat16).astype(jnp.float32)
    rest = x - one
    two = rest.astype(jnp.bfloat16).astype(jnp.float32)
    return one, two, rest - two


def prepare_kernel(
    depth_all, vol, first_slab, last_slab, center, width, density, color, light,
    cells, west, east, par, mix, center_here, width_here, density_here, color_here, light_here, sems,
):
    del first_slab, last_slab
    depth, rows, cols = vol.shape
    tiles = cols // LANES
    groups = west.shape[0]
    band = rows // groups

    def load(t, g):
        return pltpu.make_async_copy(
            vol.at[:, pl.ds(g * band, band), pl.ds(t * LANES, LANES)],
            cells.at[t, :, pl.ds(SUB + g * band, band)],
            sems.at[t * groups + g],
        )

    edges = list(dict.fromkeys((0, tiles - 1)))
    order = edges + [t for t in range(tiles) if t not in edges]
    copies = [load(t, g) for g in range(groups) for t in order]
    small = [
        pltpu.make_async_copy(src, dst, sems.at[tiles * groups + i])
        for i, (src, dst) in enumerate((
            (center, center_here), (width, width_here), (density, density_here),
            (color, color_here), (light, light_here),
        ))
    ]
    for copy in small + copies:
        copy.start()
    log2e = math.log2(math.e)

    def spread(ref, row, k, lanes=LANES):
        return jnp.broadcast_to(ref[pl.ds(row, 1), pl.ds(k, 1)], (SUB, lanes))

    border = jnp.zeros((tiles, depth, SUB, LANES), jnp.float32)
    cells[:, :, pl.ds(0, SUB), :] = border
    cells[:, :, pl.ds(SUB + rows, SUB), :] = border
    for copy in small:
        copy.wait()
    wide = lax.broadcasted_iota(jnp.int32, (SUB, MIX), 1)
    row = lax.broadcasted_iota(jnp.int32, (SUB, MIX), 0)
    piece, pair, column = wide // 16, (wide // SUB) % 2, wide % SUB
    groups_of = [[], []]
    for k in range(BUMPS):
        scale = spread(width_here, 0, k, MIX)
        middle = spread(center_here, 0, k, MIX)
        dense = spread(density_here, 0, k, MIX) * (log2e / depth_all)
        a = -log2e / (scale * scale)
        parts_a = thirds(a)
        parts_b = thirds(-2.0 * a * middle)
        parts_c = thirds(a * middle * middle + jnp.log(dense) * log2e)
        value = jnp.zeros((SUB, MIX), jnp.float32)
        for first, parts in ((0, parts_a), (6, parts_b)):
            for at, which in enumerate((0, 1, 2, 0, 1, 0)):
                value = jnp.where(piece == first + at, parts[which], value)
        value = jnp.where(column == row, value, 0.0)
        for turn in range(3):
            hit = (piece == 12) & (column == (row + turn) % SUB)
            value = jnp.where(hit, parts_c[turn], value)
        for half in range(2):
            groups_of[half].append(jnp.where(pair == half, value, 0.0))
        dense = dense[:, :LANES]
        for c in range(3):
            par[SUB + c * BUMPS + k] = spread(color_here, c, k) / dense
    for half in range(2):
        for k in range(0, BUMPS, 2):
            both = jnp.concatenate(groups_of[half][k:k + 2], axis=0)
            mix[pl.ds((half * BUMPS + k) * SUB, 2 * SUB), :] = both.astype(jnp.bfloat16)
    for a in range(3):
        par[a] = spread(light_here, 0, a) * 0.7
    lane = lax.broadcasted_iota(jnp.int32, (SUB, LANES), 1)
    per_group = band // SUB

    def extract(t, g, source, out):
        packed = jnp.zeros((SUB, LANES), jnp.float32)
        for r in range(per_group):
            for z in range(depth):
                place = r * depth + z
                tile = cells[t, z, pl.ds((g * per_group + r + 1) * SUB, SUB), :]
                shift = (place - source) % LANES
                moved = pltpu.roll(tile, shift, 1) if shift else tile
                packed = jnp.where(lane == place, moved, packed)
        out[g] = packed

    waits = iter(copies)
    for g in range(groups):
        for t in order:
            next(waits).wait()
        extract(0, g, 0, west)
        extract(tiles - 1, g, LANES - 1, east)


def prepare(depth_all, vol, *small):
    depth, rows, cols = vol.shape
    groups = -(-(rows // SUB) * depth // LANES)
    edge = jax.ShapeDtypeStruct((groups, SUB, LANES), jnp.float32)
    return pl.pallas_call(
        functools.partial(prepare_kernel, depth_all),
        out_shape=(
            jax.ShapeDtypeStruct((cols // LANES, depth, rows + 2 * SUB, LANES), jnp.float32),
            edge,
            edge,
            jax.ShapeDtypeStruct((SUB + 3 * BUMPS, SUB, LANES), jnp.float32),
            jax.ShapeDtypeStruct((2 * BUMPS * SUB, MIX), jnp.bfloat16),
        ),
        in_specs=[pl.BlockSpec(memory_space=pl.ANY)] * 8,
        out_specs=(VMEM,) * 5,
        scratch_shapes=[pltpu.VMEM(x.shape, jnp.float32) for x in small[-5:]]
        + [pltpu.SemaphoreType.DMA((cols // LANES * groups + 5,))],
        compiler_params=pltpu.CompilerParams(vmem_limit_bytes=LIMIT),
        name="prepare",
    )(vol, *small)


def split(x):
    one = x.astype(jnp.bfloat16)
    rest = x - one.astype(jnp.float32)
    two = rest.astype(jnp.bfloat16)
    return one, two, (rest - two.astype(jnp.float32)).astype(jnp.bfloat16)


def march_kernel(away, slot, extra, near, ys, zs, par, mix, cells, low, high, left, right, *refs):
    tiles, depth = cells.shape[:2]
    slab, column = lax.axis_index("depth"), lax.axis_index("col")
    here_z = lax.rem(slab, zs)
    has_low, has_high = slab > 0, slab < lax.axis_size("depth") - 1
    has_left, has_right = column > 0, column < lax.axis_size("col") - 1
    lane = lax.broadcasted_iota(jnp.int32, (SUB, LANES), 1)
    first = lane == 0
    last = lane == LANES - 1
    per_group = LANES // depth
    odd = lax.rem(here_z, 2)
    side = 2 * odd - 1
    origin, sign = (here_z - side, -side) if away else (here_z, side)
    targets = [lax.rem(origin + sign * d + zs, zs) for d in near]
    other, outs = (None, refs[extra:]) if slot is None else (refs[0], refs[1 + extra:])
    ones = jnp.ones((2 * SUB, tiles * LANES), jnp.bfloat16)
    zeros = jnp.zeros((2 * SUB, tiles * LANES), jnp.bfloat16)

    def exponents(rb, p):
        base = pl.multiple_of(rb * SUB + SUB, SUB)
        pair = jnp.concatenate([
            jnp.concatenate(
                [cells[t, 2 * p + h, pl.ds(base, SUB), :] for t in range(tiles)], axis=1
            )
            for h in range(2)
        ], axis=0)
        v1, v2, v3 = split(pair)
        q1, q2, q3 = split(pair * pair)
        return jnp.dot(
            mix[...],
            jnp.concatenate(
                [q1, q1, q1, q2, q2, q3, v1, v1, v1, v2, v2, v3, ones, zeros, zeros, zeros], axis=0
            ),
            preferred_element_type=jnp.float32,
        )

    def block(rb):
        row = pl.multiple_of(rb * SUB, SUB)
        base = pl.multiple_of(rb * SUB + SUB, SUB)

        def cell(t, z, move=0):
            if z < 0 or z >= depth:
                beyond, inside = (low, has_low) if z < 0 else (high, has_high)
                return jnp.where(inside, beyond[pl.ds(row, SUB), pl.ds(t * LANES, LANES)], 0.0)
            return cells[t, z, pl.ds(base + move, SUB), :]

        group = lax.div(rb, per_group)
        turn = lax.rem(LANES - lax.rem(rb, per_group) * depth, LANES)
        halo_left = pltpu.roll(jnp.where(has_left, left[group], 0.0), turn, 1)
        halo_right = pltpu.roll(jnp.where(has_right, right[group], 0.0), turn, 1)
        acc = [[None] * BUMPS for t in range(tiles)]
        logt = [None] * tiles
        trans = [None] * tiles
        for z in range(depth):
            if z % 2 == 0:
                power = exponents(rb, z // 2)
            here = [cell(t, z) for t in range(tiles)]
            fwd = [pltpu.roll(h, 1, 1) for h in here]
            bwd = [pltpu.roll(h, LANES - 1, 1) for h in here]
            lo = halo_left if z == 0 else pltpu.roll(halo_left, LANES - z, 1)
            hi = pltpu.roll(halo_right, LANES - 1 - z, 1)
            for t in range(tiles):
                from_left = jnp.where(first, lo if t == 0 else fwd[t - 1], fwd[t])
                from_right = jnp.where(last, hi if t == tiles - 1 else bwd[t + 1], bwd[t])
                dx = from_right - from_left
                dy = cell(t, z, 1) - cell(t, z, -1)
                dz = cell(t, z + 1) - cell(t, z - 1)
                lit = jnp.abs(par[0] * dx + par[1] * dy + par[2] * dz)
                norm = (dx * dx + dy * dy) + (dz * dz + 4.0)
                shade = 0.3 + lit * lax.rsqrt(norm)
                lanes = slice(t * LANES, (t + 1) * LANES)
                top = (z % 2) * BUMPS * SUB
                b = [
                    jnp.exp2(power[top + k * SUB:top + (k + 1) * SUB, lanes])
                    for k in range(BUMPS)
                ]
                ext = ((b[0] + b[1]) + (b[2] + b[3])) + ((b[4] + b[5]) + (b[6] + b[7]))
                logt[t] = -ext if z == 0 else logt[t] - ext
                after = jnp.exp2(logt[t])
                weight = ((1.0 if z == 0 else trans[t]) - after) * shade
                trans[t] = after
                for k in range(BUMPS):
                    term = weight * b[k]
                    acc[t][k] = term if z == 0 else acc[t][k] + term
        totals = [[] for t in range(tiles)]
        for t in range(tiles):
            for c in range(3):
                total = acc[t][0] * par[SUB + c * BUMPS]
                for k in range(1, BUMPS):
                    total = total + acc[t][k] * par[SUB + c * BUMPS + k]
                totals[t].append(total)
            totals[t].append(logt[t])
        return totals

    unroll = max(1, min(ys, BODY // len(near)))

    def step(i, unused):
        for u in range(unroll):
            j = i * unroll + u
            for q in range(len(near)):
                for t, totals in enumerate(block(j * zs + targets[q])):
                    lanes = pl.ds(t * LANES, LANES)
                    if other is not None:
                        mate = [other[slot + q, j, c, :, lanes] for c in range(4)]
                        totals = pair_over(totals, mate, odd == 1)
                    for c in range(4):
                        outs[0][q, j, c, :, lanes] = totals[c]
        return 0

    lax.fori_loop(0, ys // unroll, step, 0)


def march(name, away, near, ys, zs, par, mix, cells, low, high, left, right, other=None, after=()):
    tiles, depth = cells.shape[:2]
    work = len(near) * ys * SUB * tiles * LANES * depth
    shape = (len(near), ys, 4, SUB, tiles * LANES)
    mate, slot = ((), None) if other is None else ((other[0],), other[1])
    operands = (par, mix, cells, low, high, left, right) + mate
    return pl.pallas_call(
        functools.partial(march_kernel, away, slot, len(after), near, ys, zs),
        out_shape=jax.ShapeDtypeStruct(shape, jnp.float32),
        in_specs=[VMEM] * len(operands) + [pl.BlockSpec(memory_space=pl.ANY)] * len(after),
        out_specs=VMEM,
        compiler_params=pltpu.CompilerParams(vmem_limit_bytes=LIMIT),
        cost_estimate=pl.CostEstimate(
            flops=80 * work, bytes_accessed=4 * work, transcendentals=10 * work
        ),
        name=name,
    )(*operands, *after)


def pair_over(own, mate, mate_nearer):
    ahead = [jnp.where(mate_nearer, m, a) for a, m in zip(own, mate)]
    behind = [jnp.where(mate_nearer, a, m) for a, m in zip(own, mate)]
    seen = jnp.exp2(ahead[3])
    return [a + seen * b for a, b in zip(ahead[:3], behind[:3])] + [ahead[3] + behind[3]]


def over(parts, here):
    color, logt = [jnp.zeros_like(parts[0][0])] * 3, jnp.zeros_like(parts[0][3])
    back, back_logt = color, logt
    for s in reversed(range(len(parts))):
        turn = here == s
        back = [jnp.where(turn, a, b) for a, b in zip(color, back)]
        back_logt = jnp.where(turn, logt, back_logt)
        color = [jnp.where(turn, 0.0, a) for a in color]
        logt = jnp.where(turn, 0.0, logt)
        seen = jnp.exp2(logt)
        color = [a + seen * parts[s][c] for c, a in enumerate(color)]
        logt = logt + parts[s][3]
    seen = jnp.exp2(logt)
    return [a + seen * b for a, b in zip(color, back)], logt + back_logt


def hold(parts, work):
    anywhere = [pl.BlockSpec(memory_space=pl.ANY)] * len(parts)
    return pl.pallas_call(
        lambda *refs: None,
        out_shape=[jax.ShapeDtypeStruct(p.shape, p.dtype) for p in parts],
        in_specs=anywhere,
        out_specs=anywhere,
        input_output_aliases={i: i for i in range(len(parts))},
        compiler_params=pltpu.CompilerParams(vmem_limit_bytes=LIMIT),
        cost_estimate=pl.CostEstimate(flops=80 * work, bytes_accessed=4 * work, transcendentals=10 * work),
        name="hold",
    )(*parts)


def merge_z_kernel(ys, zs, *refs):
    pairs = zs // 2
    loose = 2 * min(2, pairs)
    singles, parts, outs = refs[:loose], refs[loose:-ys], refs[-ys:]
    me = lax.axis_index("depth")
    y, z = lax.div(me, zs), lax.rem(me, zs)
    odd = lax.rem(z, 2) == 1
    for t in range(ys):
        j = lax.rem(y + t, ys)
        held = [[p[0, j, c] for c in range(4)] for p in singles]
        held = [
            pair_over(held[i], held[i + 1], odd if i == 0 else jnp.logical_not(odd))
            for i in range(0, loose, 2)
        ]
        held += [[p[0, j, c] for c in range(4)] for p in parts]
        ring = [held[0]] + [None] * (pairs - 1)
        for r in range(1, pairs):
            even_from = 2 * r - 1 if 2 * r <= pairs else 2 * (pairs - r)
            odd_from = 2 * r if 2 * r < pairs else 2 * (pairs - r) - 1
            ring[r] = [
                jnp.where(odd, a, b) for a, b in zip(held[odd_from], held[even_from])
            ]
        color, logt = over(ring, lax.div(z, 2))
        for c in range(3):
            outs[t][c] = color[c]
        outs[t][3] = logt


def merge_z(ys, zs, parts):
    shape = parts[0].shape[2:]
    return pl.pallas_call(
        functools.partial(merge_z_kernel, ys, zs),
        out_shape=[jax.ShapeDtypeStruct(shape, jnp.float32)] * ys,
        in_specs=[VMEM] * len(parts),
        out_specs=[VMEM] * ys,
        compiler_params=pltpu.CompilerParams(vmem_limit_bytes=LIMIT),
        name="merge_z",
    )(*parts)


def merge_y_kernel(zs, *refs):
    parts, out = refs[:-1], refs[-1]
    y = lax.div(lax.axis_index("depth"), zs)
    color, logt = over([[p[c] for c in range(4)] for p in parts], y)
    for c in range(3):
        out[c] = color[c]
    out[3] = 1.0 - jnp.exp2(logt)


def merge_y(zs, parts):
    return pl.pallas_call(
        functools.partial(merge_y_kernel, zs),
        out_shape=jax.ShapeDtypeStruct(parts[0].shape, jnp.float32),
        in_specs=[VMEM] * len(parts),
        out_specs=VMEM,
        compiler_params=pltpu.CompilerParams(vmem_limit_bytes=LIMIT),
        name="merge_y",
    )(*parts)


def in_hbm(x):
    return pltpu.with_memory_space_constraint(x, pltpu.HBM)


def on_device(volume, tf_center, tf_width, tf_density, tf_color, light):
    depth, rows, cols = volume.shape
    slabs = lax.axis_size("depth")
    ys, zs = split_depth(slabs)
    depth_all = depth * slabs
    up = [(i, (i + 1) % slabs) for i in range(slabs)]
    down = [(j, i) for i, j in up]
    first_slab, last_slab = volume[0], volume[depth - 1]
    low = lax.ppermute(last_slab, "depth", up)
    high = lax.ppermute(first_slab, "depth", down)
    cells, west_edge, east_edge, par, mix = prepare(
        depth_all, in_hbm(volume), first_slab, last_slab, in_hbm(tf_center[None]),
        in_hbm(tf_width[None]), in_hbm(tf_density[None]), in_hbm(tf_color), in_hbm(light[None]),
    )
    width = lax.axis_size("col")
    east = [(i, (i + 1) % width) for i in range(width)]
    west = [(j, i) for i, j in east]
    left = lax.ppermute(east_edge, "col", east)
    right = lax.ppermute(west_edge, "col", west)

    def along_z(x, to):
        return lax.ppermute(
            x, "depth", [(y * zs + z, y * zs + to(z) % zs) for y in range(ys) for z in range(zs)]
        )

    common = (ys, zs, par, mix, cells, low, high, left, right)
    reach = (zs - 2) // 2
    far = list(range(reach, 1, -1))
    after, incoming = (), {}

    def step(name, away, near, other=None):
        nonlocal after
        parts = march(name, away, near, *common, other=other, after=after)
        after = (parts,)
        return parts

    if far:
        given = along_z(step("away", True, far), lambda z: z ^ 1)
    if reach:
        incoming["near"] = along_z(step("near", False, [1]), lambda z: z + 1 if z % 2 else z - 1)
        incoming["past"] = along_z(step("past", True, [1]), lambda z: z - 2 if z % 2 else z + 2)
    for slot, d in enumerate(far):
        parts = step("keep%d" % d, False, [d], other=(given, slot))
        incoming[d] = along_z(parts, lambda z: z + d if z % 2 else z - d)
    mate = along_z(step("mate", True, [0]), lambda z: z ^ 1)
    own = step("own", False, [0])
    for count in range(1, len(incoming) + 1):
        early = list(incoming)[:count]
        for key, part in zip(early, hold([incoming[key] for key in early], 16 * own.size)):
            incoming[key] = part
    loose = [own, mate] + ([incoming["near"], incoming["past"]] if reach else [])
    merged = list(merge_z(ys, zs, loose + [incoming[d] for d in reversed(far)]))
    for t in range(1, ys):
        pairs = [(i, (i + t * zs) % slabs) for i in range(slabs)]
        merged[t] = lax.ppermute(merged[t], "depth", pairs)
    return merge_y(zs, merged)


def solution(mesh):
    return jax.shard_map(
        on_device,
        mesh=mesh,
        in_specs=(P("depth", None, "col"), P(), P(), P(), P(), P()),
        out_specs=P(None, "depth", "col"),
        check_vma=False,
    )
```
